32 devices in a mesh: dp: 4 (over y, x), dict: 8 (over z, core).
Axes of the slice: x: 2, y: 2, z: 4, core: 2. Of those that a mesh axis runs over, the one named last changes fastest.
Arguments:
- acts: bfloat16 [2048, 8192], P('dict', 'dp'), may hold values from -6 to 6
- lists: int32 [128, 2], P('dict'), may hold values from 0 to 7, all different within a row; in each aligned block of 16 rows (0 to 15, 16 to 31, ...) at most 8 rows name the same one
- w_enc: bfloat16 [8192, 8192], P('dp', 'dict'), may hold values from -0.0625 to 0.0625
- w_dec: bfloat16 [8192, 8192], P('dict', 'dp'), may hold values from -0.1875 to 0.1875
- b_enc: bfloat16 [8192], P('dict'), may hold values from -3 to 3
- b_dec: bfloat16 [8192], P('dp'), may hold values from -3 to 3
Outputs:
- grad_enc: bfloat16 [8192, 8192], P('dp', 'dict')
- grad_dec: bfloat16 [8192, 8192], P('dict', 'dp')
The draws below stay inside these ranges and needn't reach their ends.
Inputs may be any that keep to these rules, and one draw needn't show every extreme that they name: Each row block lists 2 different panels. Among the 16 row blocks of one index of dict, no panel is listed by more than 8 blocks, and some panel is listed by exactly 8.
All inputs are finite; a program needn't handle non-finite values.
Results may differ from the reference program's by a relative error of at most 0.0057.
Values may be sent and summed in bfloat16 or wider, within the bound.
A program may use at most 128 MiB of HBM per device.

```python
import math
import jax
import jax.numpy as jnp
import numpy as np
from jax import lax

D = 8192
PANEL = 1024
ROWB = 16
BLK_DEV = 16
ACTIVE = 2
PANELS = 8
LATENTS = 8192
CAP = 8
BLOCKS = 128
ROWS = 2048
N_DICT = 8


def block_scale(rng, shape, cuts, least, largest):
    loudness = 1.0
    for position, shards_of in cuts:
        draws = jax.random.uniform(jax.random.fold_in(jax.random.fold_in(rng, 6), position), (shards_of,), jnp.float32, least / len(cuts), largest / len(cuts))
        loudness = loudness * jnp.repeat(jnp.exp(draws), shape[position] // shards_of).reshape((-1,) + (1,) * (len(shape) - 1 - position))
    return loudness


def routed_block(rng, own, number, rows, number_of, top, reach, slope):
    sequence = jax.random.permutation(rng, number_of)
    heavy_load, common = portions_of(number_of, rows * top, reach, slope, True), portions_of(number_of, rows * top, reach, slope, False)
    places = jnp.arange(number_of)

    def named(sizes, rotation):
        used = int((sizes > 0).sum())
        fixed = max(1, used // 4)
        shifted = fixed + (places - fixed + rotation * (used - fixed)) % max(1, number_of - fixed)
        return jnp.zeros((number_of,), jnp.int32).at[sequence[jnp.where(places < fixed, places, shifted)]].set(jnp.asarray(sizes, jnp.int32))

    sizes = jnp.where(number % 4 == 0, named(heavy_load, number // 4), named(common, number - number // 4 - 1))
    mixed = jax.random.permutation(jax.random.fold_in(own, 3), number_of)
    source_of, sink = mixed[0:number_of // 2 * 2:2], mixed[1:number_of // 2 * 2:2]
    margin = jnp.minimum(sizes[source_of] - 1, reach - sizes[sink]) // 2
    margin = jnp.where((source_of == sequence[0]) | (sink == sequence[0]) | (sizes[sink] == 0), 0, jnp.maximum(margin, 0))
    shifted = jax.random.randint(jax.random.fold_in(own, 4), (number_of // 2,), 0, 1 << 20) % (margin + 1)
    sizes = sizes.at[source_of].add(-shifted).at[sink].add(shifted)
    items = jnp.searchsorted(jnp.cumsum(sizes), jnp.arange(rows * top), side="right").astype(jnp.int32)
    grid = items.reshape(top, rows).T
    grid = grid[jax.random.permutation(jax.random.fold_in(own, 1), rows)]
    rotation = jax.random.randint(jax.random.fold_in(own, 2), (rows, 1), 0, top)
    return jnp.take_along_axis(grid, (jnp.arange(top)[None, :] + rotation) % top, axis=1)


def portions_of(count, total, most, lean, full):
    portions = [(1 << 20) // math.isqrt(grade ** lean) + 1 for grade in range(1, count + 1)]
    largest = most if full else min(most, max(-(-total // count), total * portions[0] // sum(portions)))
    least = 1 if total - largest >= count - 1 else 0
    counts, spare = [largest] + [least] * (count - 1), total - largest - least * (count - 1)
    while spare > 0:
        movable = [i for i in range(1, count) if counts[i] < largest] or [i for i in range(1, count) if counts[i] < most]
        mass, remaining = sum([portions[i] for i in movable]), spare
        for i in movable:
            addition = min(most - counts[i], max(1, remaining * portions[i] // mass), spare)
            counts[i] = counts[i] + addition
            spare = spare - addition
    return np.array(counts)


def normal_values(own_key, shape, width, reach, shards=(), held_as=jnp.bfloat16):
    gain = block_scale(own_key, shape, shards, -0.22, 0.18) if shards else 1.0
    result = jax.random.normal(own_key, shape, jnp.float32) * width * gain
    return jnp.minimum(jnp.maximum(result, -reach), reach).astype(held_as)


def setup_inputs(seed: int = 0) -> dict:
    keys = jax.random.split(jax.random.key(seed), 7)
    acts = normal_values(keys[0], (ROWS, D), 1.0, 6.0, ((0, 8), (1, 4)))
    lists_keys = jax.random.split(jax.random.fold_in(keys[1], 1), BLOCKS // BLK_DEV)
    lists_turns = jax.random.permutation(jax.random.fold_in(keys[1], 3), BLOCKS // BLK_DEV)
    lists = jax.vmap(lambda own, number: routed_block(jax.random.fold_in(keys[1], 2), own, number, BLK_DEV, PANELS, ACTIVE, CAP, 2))(lists_keys, lists_turns).reshape((BLOCKS, ACTIVE))
    w_enc = normal_values(keys[2], (D, LATENTS), D ** -0.5, 0.0625, ((0, 4), (1, 8)))
    w_dec = normal_values(keys[3], (LATENTS, D), PANEL ** -0.5, 0.1875, ((0, 8), (1, 4)))
    b_enc = normal_values(keys[4], (LATENTS,), 0.5, 3.0, ((0, 8),))
    b_dec = normal_values(keys[5], (D,), 0.5, 3.0, ((0, 4),))
    return {"acts": acts, "lists": lists, "w_enc": w_enc, "w_dec": w_dec, "b_enc": b_enc, "b_dec": b_dec}


def reference(acts, lists, w_enc, w_dec, b_enc, b_dec):
    blocks_x = acts.reshape(BLOCKS, ROWB, D)
    most_blocks = N_DICT * CAP

    def members(panel_id):
        listed = jnp.any(lists == panel_id, axis=1)
        member_idx = jnp.nonzero(listed, size=most_blocks, fill_value=BLOCKS)[0].astype(jnp.int32)
        valid = member_idx < BLOCKS
        safe_idx = jnp.minimum(member_idx, BLOCKS - 1).astype(jnp.int32)
        return member_idx, safe_idx, valid

    def panel_weights(panel_id):
        start = (panel_id * PANEL).astype(jnp.int32)
        enc_panel = lax.dynamic_slice_in_dim(w_enc, start, PANEL, 1)
        dec_panel = lax.dynamic_slice_in_dim(w_dec, start, PANEL, 0)
        bias_panel = lax.dynamic_slice_in_dim(b_enc, start, PANEL, 0)
        return enc_panel, dec_panel, bias_panel

    def forward(rebuilt, panel_id):
        member_idx, safe_idx, valid = members(panel_id)
        enc_panel, dec_panel, bias_panel = panel_weights(panel_id)
        rows_sel = jnp.where(valid[:, None, None], blocks_x[safe_idx], jnp.zeros((), blocks_x.dtype))
        preact = jnp.dot(rows_sel.reshape(-1, D), enc_panel, preferred_element_type=jnp.float32) + bias_panel.astype(jnp.float32)
        activity = (jnp.maximum(preact, 0.0) ** 2).astype(jnp.bfloat16)
        part = jnp.dot(activity, dec_panel, preferred_element_type=jnp.float32).astype(jnp.bfloat16)
        rebuilt = rebuilt.at[member_idx].add(part.reshape(most_blocks, ROWB, D).astype(jnp.float32), mode="drop")
        return rebuilt, (preact, activity)

    start_sum = jnp.zeros((BLOCKS, ROWB, D), jnp.float32)
    panel_ids = jnp.arange(PANELS, dtype=jnp.int32)
    rebuilt, (preacts, activities) = lax.scan(forward, start_sum, panel_ids)
    rebuilt = rebuilt + b_dec.astype(jnp.float32)
    residual_g = ((rebuilt - blocks_x.astype(jnp.float32)) * (1.0 / ROWB)).astype(jnp.bfloat16)

    def backward(inputs):
        panel_id, preact, activity = inputs
        member_idx, safe_idx, valid = members(panel_id)
        enc_panel, dec_panel, bias_panel = panel_weights(panel_id)
        rows_sel = jnp.where(valid[:, None, None], blocks_x[safe_idx], jnp.zeros((), blocks_x.dtype)).reshape(-1, D)
        resid_sel = jnp.where(valid[:, None, None], residual_g[safe_idx], jnp.zeros((), residual_g.dtype)).reshape(-1, D)
        dec_grad = jnp.dot(activity.T, resid_sel, preferred_element_type=jnp.float32).astype(jnp.bfloat16)
        dact = jnp.dot(resid_sel, dec_panel.T, preferred_element_type=jnp.float32)
        grad_pre = (dact * 2.0 * jnp.maximum(preact, 0.0)).astype(jnp.bfloat16)
        enc_grad = jnp.dot(rows_sel.T, grad_pre, preferred_element_type=jnp.float32).astype(jnp.bfloat16)
        return enc_grad, dec_grad

    enc_stack, dec_stack = lax.map(backward, (panel_ids, preacts, activities))
    grad_enc = jnp.transpose(enc_stack, (1, 0, 2)).reshape(D, LATENTS)
    grad_dec = dec_stack.reshape(LATENTS, D)
    return grad_enc, grad_dec
```

```python
import functools

import jax
import jax.numpy as jnp
from jax import lax
from jax.experimental import pallas as pl
from jax.experimental.pallas import tpu as pltpu
from jax.sharding import PartitionSpec as P

F32 = jnp.float32
BF16 = jnp.bfloat16
MESH = pl.DeviceIdType.MESH
VMEM_LIMIT = 60 * 2**20


def chip_at(k, z, nz):
    near = jnp.minimum(z, nz - 1 - z)
    odd = lax.rem(k, 2) == 1
    both = jnp.where(odd, z - (k + 1) // 2, z + k // 2)
    one = jnp.where(z <= nz - 1 - z, k, nz - 1 - k)
    return jnp.where(k <= 2 * near, both, one)


def remote(src, dst, send, recv, where):
    return pltpu.make_async_remote_copy(
        src_ref=src, dst_ref=dst, send_sem=send, recv_sem=recv,
        device_id=where, device_id_type=MESH,
    )


def greet(partners):
    barrier = pltpu.get_barrier_semaphore()
    for here, where in partners:
        @pl.when(here)
        def _():
            pl.semaphore_signal(barrier, inc=1, device_id=where, device_id_type=MESH)
    total = sum(jnp.where(here, 1, 0) for here, _ in partners)
    pl.semaphore_wait(barrier, total)


def gather_kernel(
    backward, nz, cap, rowb,
    pick_ref, shard_ref, w_ref, extra_ref, valid_ref,
    *refs,
):
    if backward:
        (rows_ref, out_ref, x_all, s1, r1, s2, r2, acc_ref, rsem, right_sem, left_sem,
         sib_sem, s1_sem, r1_sem, s2_sem, r2_sem) = refs
    else:
        (rows_ref, acc_ref, out_ref, x_all, s1, r1, s2, r2, rsem, right_sem, left_sem,
         sib_sem, s1_sem, r1_sem, s2_sem, r2_sem) = refs
    d = lax.axis_index("dp")
    me = lax.axis_index("dict")
    z, c = me // 2, lax.rem(me, 2)
    home_rows = shard_ref.shape[0]
    unit = 2 * cap * rowb
    half = s1.shape[2]
    right, left, sib = (d, me + 2), (d, me - 2), (d, me + 1 - 2 * c)
    d1 = d + 1 - 2 * lax.rem(d, 2)
    d2 = d + 2 - 4 * (d // 2)
    firsts, seconds = ((d1, me), (d2, me)), ((d2, me), (d1, me))
    true = me >= 0
    greet([(z < nz - 1, right), (z > 0, left), (true, sib), (true, (d1, me)), (true, (d2, me))])

    def span(h):
        return x_all.at[pl.ds(pl.multiple_of(h * home_rows, home_rows), home_rows)]

    def to(h, sems, where):
        return remote(span(h), span(h), sems.at[h], rsem.at[h], where)

    def forward(h, chip):
        @pl.when((chip <= z) & (z < nz - 1))
        def _():
            to(h, right_sem, right).start()

        @pl.when((chip >= z) & (z > 0))
        def _():
            to(h, left_sem, left).start()

        to(h, sib_sem, sib).start()

    def unit_rows(chip):
        return pl.ds(pl.multiple_of(chip * unit, unit), unit)

    def swap(src, dst, send, recv, part, chip, partners):
        at = unit_rows(chip)
        return remote(
            src.at[part, at], dst.at[part, at], send.at[part, chip], recv.at[part, chip],
            partners[part],
        )

    x_all[pl.ds(pl.multiple_of(me * home_rows, home_rows), home_rows), :] = shard_ref[...]

    def step(k, carry):
        @pl.when(k < nz)
        def _():
            chip = chip_at(k, z, nz)
            mine, other = 2 * chip + c, 2 * chip + 1 - c

            @pl.when(k > 0)
            def _():
                to(mine, sib_sem, sib).wait_recv()

            forward(mine, chip)
            to(other, sib_sem, sib).wait_recv()
            for core in range(2):
                h = 2 * chip + core
                home = pl.ds(pl.multiple_of(h * home_rows, home_rows), home_rows)
                slots = pl.ds(pl.multiple_of(h * cap * rowb, cap * rowb), cap * rowb)
                width = min(512, x_all.shape[1])
                for lo in range(0, x_all.shape[1], width):
                    rows_ref[slots, lo:lo + width] = jnp.dot(
                        pick_ref[h], x_all[home, lo:lo + width], preferred_element_type=F32
                    ).astype(BF16)
            at = unit_rows(chip)
            for part in range(2):
                for piece in range(2):
                    width = half // 2
                    lo = part * half + piece * width
                    if backward:
                        got = lax.dot_general(
                            rows_ref[at, :], w_ref[lo:lo + width, :], (((1,), (1,)), ((), ())),
                            preferred_element_type=F32,
                        )
                    else:
                        got = jnp.dot(
                            rows_ref[at, :], w_ref[:, lo:lo + width], preferred_element_type=F32
                        )
                    acc_ref[at, lo:lo + width] = got
                    s1[part, at, piece * width:(piece + 1) * width] = got.astype(BF16)
                swap(s1, r1, s1_sem, r1_sem, part, chip, firsts).start()

        @pl.when((k >= 1) & (k <= nz))
        def _():
            chip = chip_at(k - 1, z, nz)
            at = unit_rows(chip)
            for part in range(2):
                swap(s1, r1, s1_sem, r1_sem, part, chip, firsts).wait()
                lo = part * half
                got = acc_ref[at, lo:lo + half] + r1[part, at, :].astype(F32)
                acc_ref[at, lo:lo + half] = got
                s2[part, at, :] = got.astype(BF16)
                swap(s2, r2, s2_sem, r2_sem, part, chip, seconds).start()

        @pl.when(k >= 2)
        def _():
            chip = chip_at(k - 2, z, nz)
            at = unit_rows(chip)
            for part in range(2):
                swap(s2, r2, s2_sem, r2_sem, part, chip, seconds).wait()
                lo = part * half
                got = acc_ref[at, lo:lo + half] + r2[part, at, :].astype(F32)
                if backward:
                    out_ref[at, lo:lo + half] = (
                        got * 2.0 * extra_ref[at, lo:lo + half]
                    ).astype(BF16)
                else:
                    got = got + extra_ref[:, lo:lo + half].astype(F32)
                    got = jnp.where(valid_ref[at, :] > 0, jnp.maximum(got, 0.0), 0.0)
                    acc_ref[at, lo:lo + half] = got
                    out_ref[at, lo:lo + half] = (got * got).astype(BF16)
        return carry

    lax.fori_loop(0, nz + 2, step, 0)

    def drain(chip, carry):
        h = 2 * chip + c

        @pl.when((chip <= z) & (z < nz - 1))
        def _():
            to(h, right_sem, right).wait_send()

        @pl.when((chip >= z) & (z > 0))
        def _():
            to(h, left_sem, left).wait_send()

        to(h, sib_sem, sib).wait_send()
        return carry

    lax.fori_loop(0, nz, drain, 0)


def gather(backward, peers, cap, rowb, collective_id, pick, shard, w, extra, valid):
    nz = peers // 2
    total = peers * cap * rowb
    features = shard.shape[1]
    panel = w.shape[0] if backward else w.shape[1]
    vmem = pl.BlockSpec(memory_space=pltpu.VMEM)
    rows = jax.ShapeDtypeStruct((total, features), BF16)
    low = jax.ShapeDtypeStruct((total, panel), BF16)
    wide = jax.ShapeDtypeStruct((total, panel), F32)
    swap = pltpu.VMEM((2, total, panel // 2), BF16)
    dma = pltpu.SemaphoreType.DMA
    return pl.pallas_call(
        functools.partial(gather_kernel, backward, nz, cap, rowb),
        out_shape=(rows, low) if backward else (rows, wide, low),
        in_specs=[vmem] * 5,
        out_specs=(vmem,) * (2 if backward else 3),
        scratch_shapes=[pltpu.VMEM((peers * shard.shape[0], features), BF16)]
        + [swap] * 4
        + ([pltpu.VMEM((total, panel), F32)] if backward else [])
        + [dma((peers,))] * 4
        + [dma((2, nz))] * 4,
        compiler_params=pltpu.CompilerParams(
            collective_id=collective_id, has_side_effects=True, vmem_limit_bytes=VMEM_LIMIT
        ),
        cost_estimate=pl.CostEstimate(
            flops=2 * total * features * panel, bytes_accessed=20 * 2**20, transcendentals=0
        ),
    )(pick, shard, w, extra, valid)


def reduce_kernel(
    nz, cap, rowb,
    place_ref, act_ref, w_ref, shard_ref, bias_ref,
    out_ref, dense, sib_in, acc, line_in,
    sib_send, sib_recv, line_send, line_recv,
):
    d = lax.axis_index("dp")
    me = lax.axis_index("dict")
    z, c = me // 2, lax.rem(me, 2)
    home_rows, features = shard_ref.shape
    slots = cap * rowb
    right, left, sib = (d, me + 2), (d, me - 2), (d, me + 1 - 2 * c)
    true = me >= 0
    greet([(z < nz - 1, right), (z > 0, left), (true, sib)])
    def spread(h, target):
        at = pl.ds(pl.multiple_of(h * slots, slots), slots)
        width = min(512, features)
        for lo in range(0, features, width):
            part = jnp.dot(
                act_ref[at, :], w_ref[:, lo:lo + width], preferred_element_type=F32
            ).astype(BF16)
            target[:, lo:lo + width] = jnp.dot(
                place_ref[h], part, preferred_element_type=F32
            ).astype(BF16)

    def to_sib(chip):
        return remote(dense.at[chip], sib_in.at[chip], sib_send.at[chip], sib_recv.at[chip], sib)

    def along(chip, slot, where):
        return remote(acc.at[chip], line_in.at[slot], line_send.at[chip], line_recv.at[slot], where)

    def step(i, carry):
        chip = chip_at(nz - 1 - i, z, nz)
        spread(2 * chip + 1 - c, dense.at[chip])
        to_sib(chip).start()
        spread(2 * chip + c, acc.at[chip])
        to_sib(chip).wait_recv()

        @pl.when(chip != z)
        def _():
            behind = jnp.where(chip > z, z > 0, z < nz - 1)

            @pl.when(behind)
            def _():
                along(chip, chip, left).wait_recv()
                acc[chip] = (
                    acc[chip].astype(F32) + sib_in[chip].astype(F32) + line_in[chip].astype(F32)
                ).astype(BF16)

            @pl.when(jnp.logical_not(behind))
            def _():
                acc[chip] = (acc[chip].astype(F32) + sib_in[chip].astype(F32)).astype(BF16)

            @pl.when(chip > z)
            def _():
                along(chip, chip, right).start()

            @pl.when(chip < z)
            def _():
                slot = jnp.where(chip == z - 1, nz, chip)
                along(chip, slot, left).start()

        return carry

    lax.fori_loop(0, nz, step, 0)
    bias = bias_ref[...].astype(F32) - shard_ref[...].astype(F32)
    out_ref[...] = acc[z].astype(F32) + sib_in[z].astype(F32) + bias

    @pl.when(z > 0)
    def _():
        along(z, z, right).wait_recv()
        out_ref[...] = out_ref[...] + line_in[z].astype(F32)

    @pl.when(z < nz - 1)
    def _():
        along(z, nz, right).wait_recv()
        out_ref[...] = out_ref[...] + line_in[nz].astype(F32)

    def drain(chip, carry):
        to_sib(chip).wait_send()

        @pl.when(chip != z)
        def _():
            along(chip, chip, right).wait_send()

        return carry

    lax.fori_loop(0, nz, drain, 0)


def reduce(peers, cap, rowb, collective_id, place, act, w, shard, bias):
    nz = peers // 2
    home_rows, features = shard.shape
    vmem = pl.BlockSpec(memory_space=pltpu.VMEM)
    dma = pltpu.SemaphoreType.DMA
    one = (home_rows, features)
    return pl.pallas_call(
        functools.partial(reduce_kernel, nz, cap, rowb),
        out_shape=jax.ShapeDtypeStruct(one, F32),
        in_specs=[vmem] * 5,
        out_specs=vmem,
        scratch_shapes=[
            pltpu.VMEM((nz, *one), BF16),
            pltpu.VMEM((nz, *one), BF16),
            pltpu.VMEM((nz, *one), BF16),
            pltpu.VMEM((nz + 1, *one), BF16),
            dma((nz,)), dma((nz,)), dma((nz,)), dma((nz + 1,)),
        ],
        compiler_params=pltpu.CompilerParams(
            collective_id=collective_id, has_side_effects=True, vmem_limit_bytes=VMEM_LIMIT
        ),
        cost_estimate=pl.CostEstimate(
            flops=2 * act.shape[0] * act.shape[1] * features,
            bytes_accessed=8 * 2**20, transcendentals=0,
        ),
    )(place, act, w, shard, bias)


def on_device(acts, lists, w_enc, w_dec, b_enc, b_dec):
    peers = lax.axis_size("dict")
    me = lax.axis_index("dict")
    blocks, active = lists.shape
    rowb = acts.shape[0] // blocks
    features = acts.shape[1]
    cap = max(2, (2 * blocks * active + peers - 1) // peers)
    everyone = lax.all_gather(lists, "dict", axis=0)
    member = jnp.any(everyone == me, axis=2)
    count = member.astype(jnp.int32)
    ids = jnp.arange(blocks, dtype=jnp.int32)
    before = (ids[:, None] > ids[None, :]).astype(jnp.int32)
    rank = jnp.sum(count[:, None, :] * before[None], axis=2)
    place = jnp.where(member, rank, cap)
    match = place[:, None, :] == jnp.arange(cap, dtype=jnp.int32)[None, :, None]
    slots = jnp.sum(jnp.where(match, ids[None, None, :] + 1, 0), axis=2) - 1
    slots = jnp.repeat(slots, rowb, axis=1)
    offset = jnp.arange(cap * rowb, dtype=jnp.int32) % rowb
    source = jnp.where(slots >= 0, slots * rowb + offset[None, :], -1)
    columns = jnp.arange(acts.shape[0], dtype=jnp.int32)
    pick = (source[:, :, None] == columns[None, None, :]).astype(BF16)
    put = (columns[None, :, None] == source[:, None, :]).astype(BF16)
    valid = (source >= 0).astype(F32).reshape(-1, 1)

    rows_in, relu, act = gather(
        False, peers, cap, rowb, 0, pick, acts, w_enc, b_enc[None, :], valid
    )
    calls = max(1, peers // 8)
    width = features // calls
    pieces = []
    for i in range(calls):
        cols = slice(i * width, (i + 1) * width)
        diff = reduce(
            peers, cap, rowb, 2 + i, put, act, w_dec[:, cols], acts[:, cols], b_dec[None, cols]
        )
        pieces.append((diff * (1.0 / rowb)).astype(BF16))
    residual = pieces[0] if calls == 1 else jnp.concatenate(pieces, axis=1)
    resid_in, grad_pre = gather(
        True, peers, cap, rowb, 1, pick, residual, w_dec, relu, valid
    )
    first_rows = (((0,), (0,)), ((), ()))
    grad_dec = lax.dot_general(act, resid_in, first_rows, preferred_element_type=F32).astype(BF16)
    grad_enc = lax.dot_general(rows_in, grad_pre, first_rows, preferred_element_type=F32).astype(BF16)
    return grad_enc, grad_dec


def solution(mesh):
    in_specs = (
        P("dict", "dp"),
        P("dict", None),
        P("dp", "dict"),
        P("dict", "dp"),
        P("dict"),
        P("dp"),
    )
    out_specs = (P("dp", "dict"), P("dict", "dp"))
    return jax.shard_map(
        on_device, mesh=mesh, in_specs=in_specs, out_specs=out_specs, check_vma=False
    )
```
